32 devices in a mesh: dom: 8 (over z, y), feat: 4 (over x, core).
Axes of the slice: x: 2, y: 2, z: 4, core: 2. Of those that a mesh axis runs over, the one named last changes fastest.
Arguments:
- features: bfloat16 [3584, 128], P('dom'), may hold values from -6 to 6
- perturb: bfloat16 [3584, 128], P('dom'), may hold values from -0.5 to 0.5
- w_self: bfloat16 [128, 1024], P(None, 'feat'), may hold values from -0.5 to 0.5
- w_neigh: bfloat16 [128, 1024], P(None, 'feat'), may hold values from -0.5 to 0.5
- bias: float32 [1024], P('feat'), may hold values from -3 to 3
- upstream: bfloat16 [3584, 1024], P('dom', 'feat'), may hold values from -0.09375 to 0.09375
- hub_rows: int32 [8, 2], P('dom'), may hold values from 0 to 447, as said below
- send_rows: int32 [8, 4, 56], P('dom'), may hold values from -1 to 447, as said below
- neighbors: int32 [3584, 15], P('dom'), may hold values from 0 to 687, as said below
Outputs:
- new_perturb: bfloat16 [3584, 128], P('dom', 'feat')
- grad_self: float32 [128, 1024], P(None, 'feat')
- grad_neigh: float32 [128, 1024], P(None, 'feat')
The draws below stay inside these ranges and needn't reach their ends.
Inputs may be any that keep to these rules, and one draw needn't show every extreme that they name: hub_rows[s] are distinct rows of partition s. send_rows[s, o] lists distinct rows of partition s sent to partition s + off(o) mod 8; live entries come first, at least 14 of them, and in every draw some list is full with 56 live entries. `neighbors`: indices below 448 are rows of the node's own partition; indices 448 + o * 56 + j refer only to live slots of the list that partition s = p - off(o) mod 8 sends to p; indices from 672 on are hub nodes.
All inputs are finite; a program needn't handle non-finite values.
Results may differ from the reference program's by a relative error of at most 0.001.
The reference program's roundings to bfloat16 on the way (of `perturbed`, `halo`, `hubs`, `table`, `neighbor_mean` and `grad_pre`) count: a program that leaves them out, or rounds other values in their place, can miss the bound.
Values may be sent and summed in bfloat16 or wider, within the bound.
A program may use at most 64 MiB of HBM per device.

```python
import jax
import jax.numpy as jnp
from jax import lax

F_IN = 128
HIDDEN_SIZE = 1024
K = 15
R = 448
NOFF = 4
SLOT = 56
HUB_DEV = 2
DOMAINS = 8
NODES = 3584
HUBS = 16
TABLE = 688


def halo_counts(key):
    counts = jax.random.randint(jax.random.fold_in(key, 11), (DOMAINS * NOFF,), SLOT // 4, SLOT + 1)
    chosen = jax.random.randint(jax.random.fold_in(key, 12), (), 0, DOMAINS * NOFF)
    counts = jnp.where(jnp.arange(DOMAINS * NOFF) == chosen, SLOT, counts)
    return counts.reshape(DOMAINS, NOFF).astype(jnp.int32)


def draw_send_rows(key, part):
    counts = halo_counts(key)
    keys = jax.random.split(jax.random.fold_in(key, 13), DOMAINS * NOFF)
    shuffled = jax.vmap(lambda one: jax.random.permutation(one, R)[:SLOT])(keys)
    shuffled = shuffled.reshape(DOMAINS, NOFF, SLOT).astype(jnp.int32)
    slot_ids = jnp.arange(SLOT, dtype=jnp.int32)
    return jnp.where(slot_ids[None, None, :] < counts[:, :, None], shuffled, -1).astype(jnp.int32)


def draw_hub_rows(key, part):
    keys = jax.random.split(jax.random.fold_in(key, 14), DOMAINS)
    chosen = jax.vmap(lambda one: jax.random.permutation(one, R)[:HUB_DEV])(keys).astype(jnp.int32)
    top_part = jax.random.randint(jax.random.fold_in(key, 20), (), 0, DOMAINS)
    low_part = (top_part + 1) % DOMAINS
    top_list = chosen[top_part]
    top_list = jnp.where(top_list == R - 1, top_list[0], top_list).at[0].set(R - 1)
    low_list = chosen[low_part]
    low_list = jnp.where(low_list == 0, low_list[0], low_list).at[0].set(0)
    chosen = chosen.at[top_part].set(top_list)
    chosen = chosen.at[low_part].set(low_list)
    return chosen.astype(jnp.int32)


def draw_neighbors(key, part):
    counts = halo_counts(key)
    category = jax.random.randint(jax.random.fold_in(key, 15), (NODES, K), 0, 4)
    local_row = jax.random.randint(jax.random.fold_in(key, 16), (NODES, K), 0, R)
    direction = jax.random.randint(jax.random.fold_in(key, 17), (NODES, K), 0, NOFF)
    part_of = (jnp.arange(NODES, dtype=jnp.int32) // R)[:, None]
    offset = jnp.where(direction < 2, direction - 2, direction - 1)
    source_part = (part_of - offset) % DOMAINS
    live_count = counts[source_part, direction]
    slot_pick = jax.random.randint(jax.random.fold_in(key, 18), (NODES, K), 0, 2 ** 20) % live_count
    hub_pick = jax.random.randint(jax.random.fold_in(key, 19), (NODES, K), 0, HUBS)
    halo_index = R + direction * SLOT + slot_pick
    hub_index = R + NOFF * SLOT + hub_pick
    return jnp.where(category < 2, local_row, jnp.where(category == 2, halo_index, hub_index)).astype(jnp.int32)


def steps_of(key, extent, cuts, smallest, largest):
    def one(dim, parts):
        steps = jax.random.uniform(jax.random.fold_in(jax.random.fold_in(key, 6), dim), (parts,), jnp.float32, smallest / len(cuts), largest / len(cuts))
        return jnp.repeat(jnp.exp(steps), extent[dim] // parts).reshape((-1,) + (1,) * (len(extent) - dim - 1))

    loudness = one(*cuts[0])
    for cut in cuts[1:]:
        loudness = loudness * one(*cut)
    return loudness


def noise(own_key, extent, width, limit, cuts=(), kind=jnp.bfloat16):
    result = jax.random.normal(own_key, extent, jnp.float32) * width
    if len(cuts) > 0:
        result = steps_of(own_key, extent, cuts, -0.22, 0.18) * result
    return jnp.clip(result, min=-limit, max=limit).astype(kind)


def setup_inputs(seed: int = 0) -> dict:
    streams_of = jax.random.split(jax.random.key(seed), 10)
    features = noise(streams_of[0], (NODES, F_IN), 1.0, 6.0, ((0, 8),))
    perturb = jnp.clip(jax.random.uniform(streams_of[1], (NODES, F_IN), jnp.float32, -0.5, 0.5) * steps_of(streams_of[1], (NODES, F_IN), ((0, 8),), -0.4, 0.0), -0.5, 0.5).astype(jnp.bfloat16)
    w_self = noise(streams_of[2], (F_IN, HIDDEN_SIZE), F_IN ** -0.5, 0.5, ((1, 4),))
    w_neigh = noise(streams_of[3], (F_IN, HIDDEN_SIZE), F_IN ** -0.5, 0.5, ((1, 4),))
    bias = noise(streams_of[4], (HIDDEN_SIZE,), 0.5, 3.0, ((0, 4),), jnp.float32)
    upstream = noise(streams_of[5], (NODES, HIDDEN_SIZE), NODES ** -0.5, 0.09375, ((0, 8), (1, 4)))
    hub_rows = draw_hub_rows(jax.random.fold_in(streams_of[9], 71), 0)
    send_rows = draw_send_rows(jax.random.fold_in(streams_of[9], 71), 0)
    neighbors = draw_neighbors(jax.random.fold_in(streams_of[9], 71), 0)
    return {"features": features, "perturb": perturb, "w_self": w_self, "w_neigh": w_neigh, "bias": bias, "upstream": upstream, "hub_rows": hub_rows, "send_rows": send_rows, "neighbors": neighbors}


def offset_of(direction):
    return direction - 2 if direction < 2 else direction - 1

def dense_part(blocks, w_self, w_neigh, bias):
    own_rows, mean_rows, cotangent = blocks
    preact = jnp.dot(own_rows, w_self, preferred_element_type=jnp.float32)
    preact = preact + jnp.dot(mean_rows, w_neigh, preferred_element_type=jnp.float32) + bias
    sigmoid_pre = jax.nn.sigmoid(preact)
    grad_pre = (cotangent.astype(jnp.float32) * sigmoid_pre * (1.0 + preact * (1.0 - sigmoid_pre))).astype(jnp.bfloat16)
    own_grad = jnp.dot(grad_pre, w_self.T, preferred_element_type=jnp.float32)
    spread = jnp.dot(grad_pre, w_neigh.T, preferred_element_type=jnp.float32) / K
    part_self = jnp.dot(own_rows.T, grad_pre, preferred_element_type=jnp.float32)
    part_neigh = jnp.dot(mean_rows.T, grad_pre, preferred_element_type=jnp.float32)
    return (own_grad, spread, part_self, part_neigh)

def reference(features, perturb, w_self, w_neigh, bias, upstream, hub_rows, send_rows, neighbors):
    perturbed = (features.astype(jnp.float32) + perturb.astype(jnp.float32)).astype(jnp.bfloat16)
    dom_ids = jnp.arange(DOMAINS, dtype=jnp.int32)
    halo_pieces = []
    for direction in range(NOFF):
        source_part = (dom_ids - offset_of(direction)) % DOMAINS
        row_list = send_rows[source_part, direction]
        flat_index = source_part[:, None] * R + jnp.maximum(row_list, 0)
        picked = perturbed[flat_index]
        halo_pieces.append(jnp.where((row_list >= 0)[:, :, None], picked, jnp.zeros((), jnp.bfloat16)))
    halo = jnp.concatenate(halo_pieces, axis=1)
    hub_index = (dom_ids[:, None] * R + hub_rows).reshape(-1)
    hubs = perturbed[hub_index]
    table = jnp.concatenate([perturbed.reshape(DOMAINS, R, F_IN), halo, jnp.broadcast_to(hubs[None], (DOMAINS, HUBS, F_IN))], axis=1)
    flat_table = table.reshape(DOMAINS * TABLE, F_IN)
    table_index = (jnp.arange(NODES, dtype=jnp.int32) // R * TABLE)[:, None] + neighbors
    gathered_sum = jnp.zeros((NODES, F_IN), jnp.float32)
    for position in range(K):
        gathered_sum = gathered_sum + flat_table[table_index[:, position]].astype(jnp.float32)
    neighbor_mean = (gathered_sum / K).astype(jnp.bfloat16)
    blocks = (perturbed.reshape(DOMAINS, R, F_IN), neighbor_mean.reshape(DOMAINS, R, F_IN), upstream.reshape(DOMAINS, R, HIDDEN_SIZE))
    own_grad, spread, part_self, part_neigh = lax.map(lambda blk: dense_part(blk, w_self, w_neigh, bias), blocks)
    grad_self = lax.optimization_barrier(jnp.sum(part_self, axis=0))
    grad_neigh = lax.optimization_barrier(jnp.sum(part_neigh, axis=0))
    own_grad = own_grad.reshape(NODES, F_IN)
    spread = spread.reshape(NODES, F_IN)
    table_grad = jnp.zeros((DOMAINS * TABLE, F_IN), jnp.float32)
    for position in range(K):
        table_grad = table_grad.at[table_index[:, position]].add(spread)
    table_grad = table_grad.reshape(DOMAINS, TABLE, F_IN)
    grad_in = own_grad + table_grad[:, :R].reshape(NODES, F_IN)
    for direction in range(NOFF):
        source_part = (dom_ids - offset_of(direction)) % DOMAINS
        row_list = send_rows[source_part, direction]
        target_index = jnp.where(row_list >= 0, source_part[:, None] * R + row_list, NODES)
        returned = table_grad[:, R + direction * SLOT:R + (direction + 1) * SLOT]
        grad_in = grad_in.at[target_index.reshape(-1)].add(returned.reshape(-1, F_IN), mode='drop')
    hub_total = lax.optimization_barrier(jnp.sum(table_grad[:, R + NOFF * SLOT:], axis=0))
    grad_in = grad_in.at[hub_index].add(hub_total)
    mean_square = lax.optimization_barrier(jnp.mean(grad_in * grad_in, axis=1, keepdims=True))
    new_perturb = (perturb.astype(jnp.float32) + 0.5 * grad_in / jnp.sqrt(mean_square + 1e-06)).astype(jnp.bfloat16)
    return (new_perturb, grad_self, grad_neigh)
```

```python
import functools

import jax
import jax.numpy as jnp
from jax import lax
from jax.experimental import pallas as pl
from jax.experimental.pallas import tpu as pltpu
from jax.sharding import PartitionSpec as P

K = 15
NOFF = 4
HUB_SLOT = 8
ROW_TILE = 16
BUILD = 32
MESH = pl.DeviceIdType.MESH
F32 = jnp.float32
BF16 = jnp.bfloat16


def offset_of(direction):
    return direction - 2 if direction < 2 else direction - 1


def dot(left, right, dims):
    return lax.dot_general(left, right, (dims, ((), ())), preferred_element_type=F32)


NN = ((1,), (0,))
NT = ((1,), (1,))


def halves(value, axis):
    high = value.astype(BF16)
    low = (value - high.astype(F32)).astype(BF16)
    return jnp.concatenate([high, low], axis)


def each(count, body):
    if count <= 8:
        for step in range(count):
            body(step)
    else:

        def run(step, carry):
            body(step)
            return carry

        lax.fori_loop(0, count, run, 0)


def kernel(
    doms,
    feats,
    owners,
    slots,
    features,
    perturb,
    w_self,
    w_neigh,
    bias,
    upstream,
    hub_rows,
    send_rows,
    neighbors,
    new_perturb,
    grad_self,
    grad_neigh,
    lists,
    counts,
    perturb_t,
    halo_out,
    halo_in,
    hub_out,
    hub_in,
    back_out,
    back_in,
    hubg_out,
    hubg_in,
    part_out,
    part_in,
    whole,
    cols_out,
    cols_in,
    sq_out,
    sq_in,
    halo_s,
    halo_r,
    hub_s,
    hub_r,
    back_s,
    back_r,
    hubg_s,
    hubg_r,
    part_s,
    part_r,
    whole_s,
    whole_r,
    cols_s,
    cols_r,
    sq_s,
    sq_r,
):
    me = lax.axis_index("dom")
    col = lax.axis_index("feat")
    rows, width = features.shape
    slot_pad = halo_out.shape[1]
    halo_rows = NOFF * slot_pad
    chunk = part_out.shape[1]

    def dom_peer(step):
        return lax.rem(me + step + 1, doms)

    def feat_peer(step):
        return lax.rem(col + step + 1, feats)

    def at_offset(by):
        return lax.rem(me + by + doms, doms)

    barrier = pltpu.get_barrier_semaphore()

    def greet_dom(step):
        pl.semaphore_signal(
            barrier, inc=1, device_id=(dom_peer(step), col), device_id_type=MESH
        )

    def greet_feat(step):
        pl.semaphore_signal(
            barrier, inc=1, device_id=(me, feat_peer(step)), device_id_type=MESH
        )

    each(doms - 1, greet_dom)
    each(feats - 1, greet_feat)

    def copy_to(src, dst, send, recv, dom, feat):
        return pltpu.make_async_remote_copy(
            src_ref=src,
            dst_ref=dst,
            send_sem=send,
            recv_sem=recv,
            device_id=(dom, feat),
            device_id_type=MESH,
        )

    perturb_f32 = perturb[...].astype(F32)
    perturbed = (features[...].astype(F32) + perturb_f32).astype(BF16)
    lists[...] = jnp.full(lists.shape, -1, jnp.int32)
    lists[0:NOFF, 0:slots] = send_rows[0]
    lists[NOFF : NOFF + 1, 0 : hub_rows.shape[1]] = hub_rows[...]
    by_slot = jnp.transpose(lists[...].astype(F32))
    row_ids = lax.broadcasted_iota(jnp.int32, (slot_pad, rows), 1).astype(F32)
    picks = [
        jnp.where(by_slot[0:slot_pad, o : o + 1] == row_ids, 1.0, 0.0).astype(BF16)
        for o in range(NOFF)
    ]
    pick_halo = jnp.concatenate(picks, 0)
    pick_hub = jnp.where(
        by_slot[0:ROW_TILE, NOFF : NOFF + 1] == row_ids[0:ROW_TILE], 1.0, 0.0
    ).astype(BF16)
    picked = dot(pick_halo, perturbed, NN).astype(BF16)
    for o in range(NOFF):
        halo_out[o] = picked[o * slot_pad : (o + 1) * slot_pad]
    own_hubs = dot(pick_hub, perturbed, NN)[0:HUB_SLOT]
    hub_out[...] = own_hubs
    hub_in[me] = own_hubs

    pl.semaphore_wait(barrier, doms - 1 + feats - 1)

    def halo_copy(o):
        return copy_to(
            halo_out.at[o], halo_in.at[o], halo_s.at[o], halo_r.at[o], at_offset(offset_of(o)), col
        )

    def hub_send(step):
        peer = dom_peer(step)
        return copy_to(hub_out, hub_in.at[me], hub_s.at[peer], hub_r.at[me], peer, col)

    def hub_recv(step):
        peer = dom_peer(step)
        return copy_to(hub_out, hub_in.at[peer], hub_s.at[peer], hub_r.at[peer], peer, col)

    for o in range(NOFF):
        halo_copy(o).start()
    each(doms - 1, lambda step: hub_send(step).start())

    nodes = neighbors[...]
    far = nodes - rows
    shifted = nodes
    for o in range(1, NOFF):
        shifted = shifted + jnp.where(far >= o * slots, slot_pad - slots, 0)
    hub_id = far - NOFF * slots
    hub_at = rows + halo_rows + (hub_id >> 1) * HUB_SLOT + (hub_id & 1)
    place = jnp.where(hub_id >= 0, hub_at, shifted)

    def build(block, carry):
        first = pl.multiple_of(block * BUILD, BUILD)
        ids = lax.broadcasted_iota(jnp.int32, (BUILD, rows), 0) + first
        total = jnp.zeros((BUILD, rows), F32)
        for k in range(K):
            total = total + jnp.where(place[k : k + 1] == ids, 1.0, 0.0)
        counts[pl.ds(first, BUILD)] = total.astype(BF16)
        return carry

    lax.fori_loop(0, counts.shape[0] // BUILD, build, 0)

    turned = jnp.transpose(perturb_f32)
    for g in range(feats):
        perturb_t[g] = turned[g * (width // feats) : (g + 1) * (width // feats)]
    perturbed_t = jnp.transpose(perturbed.astype(F32)).astype(BF16)
    summed_t = dot(perturbed_t, counts[0:rows], NN)
    preact_self = dot(perturbed, w_self[...], NN) + bias[...]

    for o in range(NOFF):
        halo_copy(o).wait_recv()
    each(doms - 1, lambda step: hub_recv(step).wait_recv())
    remote = jnp.concatenate(
        [halo_in[...].astype(F32).reshape(halo_rows, width), hub_in[...].reshape(-1, width)], 0
    )
    remote_t = jnp.transpose(remote).astype(BF16)
    summed_t = summed_t + dot(remote_t, counts[rows:], NN)
    mean_t = summed_t / K
    mean = jnp.transpose(mean_t).astype(BF16)
    preact = preact_self + dot(mean, w_neigh[...], NN)
    sigmoid_pre = jax.nn.sigmoid(preact)
    grad_pre = (
        upstream[...].astype(F32) * sigmoid_pre * (1.0 + preact * (1.0 - sigmoid_pre))
    ).astype(BF16)

    spread_t = halves(dot(w_neigh[...], grad_pre, NT) / K, 0)
    back = dot(counts[rows:], spread_t, NT)
    back = back[:, 0:width] + back[:, width:]
    for o in range(NOFF):
        back_out[o] = back[o * slot_pad : (o + 1) * slot_pad]
    hubg_out[...] = back[halo_rows:].reshape(hubg_out.shape)

    def back_copy(o):
        return copy_to(
            back_out.at[o], back_in.at[o], back_s.at[o], back_r.at[o], at_offset(-offset_of(o)), col
        )

    def hubg_send(step):
        peer = dom_peer(step)
        return copy_to(
            hubg_out.at[peer], hubg_in.at[me], hubg_s.at[peer], hubg_r.at[me], peer, col
        )

    def hubg_recv(step):
        peer = dom_peer(step)
        return copy_to(
            hubg_out.at[peer], hubg_in.at[peer], hubg_s.at[peer], hubg_r.at[peer], peer, col
        )

    for o in range(NOFF):
        back_copy(o).start()
    each(doms - 1, lambda step: hubg_send(step).start())

    both_t = jnp.concatenate([perturbed_t, mean_t.astype(BF16)], 0)
    weight_grads = dot(both_t, grad_pre, NN)
    for i in range(owners):
        part_out[i] = weight_grads[i * chunk : (i + 1) * chunk]

    def on_owner(dom, body):
        if owners == doms:
            body()
        else:
            pl.when(dom < owners)(body)

    def part_send(step):
        peer = dom_peer(step)
        return copy_to(part_out.at[peer], part_in.at[me], part_s.at[peer], part_r.at[me], peer, col)

    def part_recv(step):
        peer = dom_peer(step)
        return copy_to(part_out.at[0], part_in.at[peer], part_s.at[peer], part_r.at[peer], peer, col)

    def whole_send(step):
        peer = dom_peer(step)
        return copy_to(whole.at[me], whole.at[me], whole_s.at[peer], whole_r.at[me], peer, col)

    def whole_recv(step):
        peer = dom_peer(step)
        return copy_to(whole.at[peer], whole.at[peer], whole_s.at[peer], whole_r.at[peer], peer, col)

    each(doms - 1, lambda step: on_owner(dom_peer(step), lambda: part_send(step).start()))

    local = dot(spread_t, counts[0:rows], NT)
    grad_t = dot(w_self[...], grad_pre, NT) + local[0:width] + local[width:]

    for o in range(NOFF):
        back_copy(o).wait_recv()
    each(doms - 1, lambda step: hubg_recv(step).wait_recv())
    hubg_in[me] = hubg_out[me]
    hub_sum = jnp.sum(hubg_in[...], 0)
    hub_sum = jnp.concatenate([hub_sum, jnp.zeros((ROW_TILE - HUB_SLOT, width), F32)], 0)
    returned_t = halves(jnp.transpose(back_in[...].reshape(halo_rows, width)), 0)
    hub_sum_t = halves(jnp.transpose(hub_sum), 0)
    added = dot(returned_t, pick_halo, NN) + dot(hub_sum_t, pick_hub, NN)
    grad_t = grad_t + added[0:width] + added[width:]
    part_width = width // feats
    for g in range(feats):
        cols_out[g] = grad_t[g * part_width : (g + 1) * part_width]

    def cols_send(step):
        peer = feat_peer(step)
        return copy_to(cols_out.at[peer], cols_in.at[col], cols_s.at[peer], cols_r.at[col], me, peer)

    def cols_recv(step):
        peer = feat_peer(step)
        return copy_to(
            cols_out.at[peer], cols_in.at[peer], cols_s.at[peer], cols_r.at[peer], me, peer
        )

    each(feats - 1, lambda step: cols_send(step).start())

    def sum_parts():
        each(doms - 1, lambda step: part_recv(step).wait_recv())
        part_in[me] = part_out[me]
        whole[me] = jnp.sum(part_in[...], 0)
        each(doms - 1, lambda step: whole_send(step).start())

    on_owner(me, sum_parts)

    each(feats - 1, lambda step: cols_recv(step).wait_recv())
    cols_in[col] = cols_out[col]
    grad_cols = jnp.sum(cols_in[...], 0)
    square = jnp.sum(grad_cols * grad_cols, 0, keepdims=True)
    sq_out[...] = jnp.broadcast_to(square, sq_out.shape)

    def sq_send(step):
        peer = feat_peer(step)
        return copy_to(sq_out, sq_in.at[col], sq_s.at[peer], sq_r.at[col], me, peer)

    def sq_recv(step):
        peer = feat_peer(step)
        return copy_to(sq_out, sq_in.at[peer], sq_s.at[peer], sq_r.at[peer], me, peer)

    each(feats - 1, lambda step: sq_send(step).start())
    each(feats - 1, lambda step: sq_recv(step).wait_recv())
    sq_in[col] = sq_out[...]
    mean_square = jnp.sum(sq_in[...], 0)[0:1] / width
    stepped = perturb_t[col] + 0.5 * grad_cols / jnp.sqrt(mean_square + 1e-06)
    finish(new_perturb, stepped)

    def take_whole(step):
        on_owner(dom_peer(step), lambda: whole_recv(step).wait_recv())

    each(doms - 1, take_whole)
    half = owners // 2
    grad_self[...] = whole[0:half].reshape(grad_self.shape)
    grad_neigh[...] = whole[half:owners].reshape(grad_neigh.shape)

    for o in range(NOFF):
        halo_copy(o).wait_send()
        back_copy(o).wait_send()
    each(doms - 1, lambda step: hub_send(step).wait_send())
    each(doms - 1, lambda step: hubg_send(step).wait_send())
    each(doms - 1, lambda step: on_owner(dom_peer(step), lambda: part_send(step).wait_send()))
    on_owner(me, lambda: each(doms - 1, lambda step: whole_send(step).wait_send()))
    each(feats - 1, lambda step: cols_send(step).wait_send())
    each(feats - 1, lambda step: sq_send(step).wait_send())


def finish(new_perturb, stepped):
    new_perturb[...] = stepped.astype(BF16)


def per_device(
    doms, feats, features, perturb, w_self, w_neigh, bias, upstream, hub_rows, send_rows, neighbors
):
    rows, width = features.shape
    hidden = w_self.shape[1]
    slots = send_rows.shape[2]
    slot_pad = (slots + ROW_TILE - 1) // ROW_TILE * ROW_TILE
    chunk = max(8, 2 * width // doms)
    owners = 2 * width // chunk
    table = rows + NOFF * slot_pad + doms * HUB_SLOT
    part_width = width // feats
    vmem = pl.BlockSpec(memory_space=pltpu.VMEM)
    sems = pltpu.SemaphoreType.DMA
    scratch = [
        pltpu.VMEM((8, 128), jnp.int32),
        pltpu.VMEM((table, rows), BF16),
        pltpu.VMEM((feats, part_width, rows), F32),
        pltpu.VMEM((NOFF, slot_pad, width), BF16),
        pltpu.VMEM((NOFF, slot_pad, width), BF16),
        pltpu.VMEM((HUB_SLOT, width), F32),
        pltpu.VMEM((doms, HUB_SLOT, width), F32),
        pltpu.VMEM((NOFF, slot_pad, width), F32),
        pltpu.VMEM((NOFF, slot_pad, width), F32),
        pltpu.VMEM((doms, HUB_SLOT, width), F32),
        pltpu.VMEM((doms, HUB_SLOT, width), F32),
        pltpu.VMEM((owners, chunk, hidden), F32),
        pltpu.VMEM((doms, chunk, hidden), F32),
        pltpu.VMEM((owners, chunk, hidden), F32),
        pltpu.VMEM((feats, part_width, rows), F32),
        pltpu.VMEM((feats, part_width, rows), F32),
        pltpu.VMEM((8, rows), F32),
        pltpu.VMEM((feats, 8, rows), F32),
        sems((NOFF,)),
        sems((NOFF,)),
        sems((doms,)),
        sems((doms,)),
        sems((NOFF,)),
        sems((NOFF,)),
        sems((doms,)),
        sems((doms,)),
        sems((doms,)),
        sems((doms,)),
        sems((doms,)),
        sems((doms,)),
        sems((feats,)),
        sems((feats,)),
        sems((feats,)),
        sems((feats,)),
    ]
    new_t, grad_self, grad_neigh = pl.pallas_call(
        functools.partial(kernel, doms, feats, owners, slots),
        out_shape=(
            jax.ShapeDtypeStruct((part_width, rows), BF16),
            jax.ShapeDtypeStruct((width, hidden), F32),
            jax.ShapeDtypeStruct((width, hidden), F32),
        ),
        in_specs=[vmem] * 9,
        out_specs=(vmem,) * 3,
        scratch_shapes=scratch,
        compiler_params=pltpu.CompilerParams(
            collective_id=0, has_side_effects=True, vmem_limit_bytes=40 * 2**20
        ),
    )(
        features,
        perturb,
        w_self,
        w_neigh,
        bias.reshape(1, hidden),
        upstream,
        hub_rows,
        send_rows,
        neighbors.T,
    )
    return new_t.T, grad_self, grad_neigh


def solution(mesh):
    in_specs = (
        P("dom", None),
        P("dom", None),
        P(None, "feat"),
        P(None, "feat"),
        P("feat"),
        P("dom", "feat"),
        P("dom", None),
        P("dom", None, None),
        P("dom", None),
    )
    out_specs = (P("dom", "feat"), P(None, "feat"), P(None, "feat"))
    return jax.shard_map(
        functools.partial(per_device, mesh.shape["dom"], mesh.shape["feat"]),
        mesh=mesh,
        in_specs=in_specs,
        out_specs=out_specs,
        check_vma=False,
    )
```

```python
import functools

import jax
import jax.numpy as jnp
from jax import lax
from jax.experimental import pallas as pl
from jax.experimental.pallas import tpu as pltpu
from jax.sharding import PartitionSpec as P

K = 15
NOFF = 4
HUB_SLOT = 8
ROW_TILE = 16
BUILD = 32
MESH = pl.DeviceIdType.MESH
F32 = jnp.float32
BF16 = jnp.bfloat16


def offset_of(direction):
    return direction - 2 if direction < 2 else direction - 1


def dot(left, right, dims):
    return lax.dot_general(left, right, (dims, ((), ())), preferred_element_type=F32)


NN = ((1,), (0,))
NT = ((1,), (1,))


def halves(value, axis):
    high = value.astype(BF16)
    low = (value - high.astype(F32)).astype(BF16)
    return jnp.concatenate([high, low], axis)


def each(count, body):
    if count <= 8:
        for step in range(count):
            body(step)
    else:

        def run(step, carry):
            body(step)
            return carry

        lax.fori_loop(0, count, run, 0)


def kernel(
    doms,
    feats,
    owners,
    slots,
    features_far,
    perturb_far,
    send_rows_far,
    hub_rows_far,
    neighbors_far,
    w_self_far,
    bias_far,
    w_neigh_far,
    upstream_far,
    new_perturb,
    grad_self,
    grad_neigh,
    lists,
    counts,
    perturb_t,
    halo_out,
    halo_in,
    hub_out,
    hub_in,
    back_out,
    back_in,
    hubg_out,
    hubg_in,
    part_out,
    part_in,
    whole,
    cols_out,
    cols_in,
    sq_out,
    sq_in,
    halo_s,
    halo_r,
    hub_s,
    hub_r,
    back_s,
    back_r,
    hubg_s,
    hubg_r,
    part_s,
    part_r,
    whole_s,
    whole_r,
    cols_s,
    cols_r,
    sq_s,
    sq_r,
    features,
    perturb,
    send_rows,
    hub_rows,
    neighbors,
    w_self,
    bias,
    w_neigh,
    upstream,
    load_s,
):
    far = (
        features_far,
        perturb_far,
        send_rows_far,
        hub_rows_far,
        neighbors_far,
        w_self_far,
        bias_far,
        w_neigh_far,
        upstream_far,
    )
    near = (features, perturb, send_rows, hub_rows, neighbors, w_self, bias, w_neigh, upstream)
    loads = [
        pltpu.make_async_copy(there, here, load_s.at[i])
        for i, (there, here) in enumerate(zip(far, near))
    ]
    for load in loads:
        load.start()
    me = lax.axis_index("dom")
    col = lax.axis_index("feat")
    rows, width = features.shape
    slot_pad = halo_out.shape[1]
    halo_rows = NOFF * slot_pad
    chunk = part_out.shape[1]

    def dom_peer(step):
        return lax.rem(me + step + 1, doms)

    def feat_peer(step):
        return lax.rem(col + step + 1, feats)

    def at_offset(by):
        return lax.rem(me + by + doms, doms)

    barrier = pltpu.get_barrier_semaphore()

    def greet_dom(step):
        pl.semaphore_signal(
            barrier, inc=1, device_id=(dom_peer(step), col), device_id_type=MESH
        )

    def greet_feat(step):
        pl.semaphore_signal(
            barrier, inc=1, device_id=(me, feat_peer(step)), device_id_type=MESH
        )

    each(doms - 1, greet_dom)
    each(feats - 1, greet_feat)

    def copy_to(src, dst, send, recv, dom, feat):
        return pltpu.make_async_remote_copy(
            src_ref=src,
            dst_ref=dst,
            send_sem=send,
            recv_sem=recv,
            device_id=(dom, feat),
            device_id_type=MESH,
        )

    for load in loads[0:4]:
        load.wait()
    perturb_f32 = perturb[...].astype(F32)
    perturbed = (features[...].astype(F32) + perturb_f32).astype(BF16)
    lists[...] = jnp.full(lists.shape, -1, jnp.int32)
    lists[0:NOFF, 0:slots] = send_rows[0]
    lists[NOFF : NOFF + 1, 0 : hub_rows.shape[1]] = hub_rows[...]
    by_slot = jnp.transpose(lists[...].astype(F32))
    row_ids = lax.broadcasted_iota(jnp.int32, (slot_pad, rows), 1).astype(F32)
    picks = [
        jnp.where(by_slot[0:slot_pad, o : o + 1] == row_ids, 1.0, 0.0).astype(BF16)
        for o in range(NOFF)
    ]
    pick_halo = jnp.concatenate(picks, 0)
    pick_hub = jnp.where(
        by_slot[0:ROW_TILE, NOFF : NOFF + 1] == row_ids[0:ROW_TILE], 1.0, 0.0
    ).astype(BF16)
    picked = dot(pick_halo, perturbed, NN).astype(BF16)
    for o in range(NOFF):
        halo_out[o] = picked[o * slot_pad : (o + 1) * slot_pad]
    own_hubs = dot(pick_hub, perturbed, NN)[0:HUB_SLOT]
    hub_out[...] = own_hubs
    hub_in[me] = own_hubs

    pl.semaphore_wait(barrier, doms - 1 + feats - 1)

    def halo_copy(o):
        return copy_to(
            halo_out.at[o], halo_in.at[o], halo_s.at[o], halo_r.at[o], at_offset(offset_of(o)), col
        )

    def hub_send(step):
        peer = dom_peer(step)
        return copy_to(hub_out, hub_in.at[me], hub_s.at[peer], hub_r.at[me], peer, col)

    def hub_recv(step):
        peer = dom_peer(step)
        return copy_to(hub_out, hub_in.at[peer], hub_s.at[peer], hub_r.at[peer], peer, col)

    for o in range(NOFF):
        halo_copy(o).start()
    each(doms - 1, lambda step: hub_send(step).start())

    for load in loads[4:7]:
        load.wait()
    nodes = neighbors[...]
    beyond = nodes - rows
    shifted = nodes
    for o in range(1, NOFF):
        shifted = shifted + jnp.where(beyond >= o * slots, slot_pad - slots, 0)
    hub_id = beyond - NOFF * slots
    hub_at = rows + halo_rows + (hub_id >> 1) * HUB_SLOT + (hub_id & 1)
    place = jnp.where(hub_id >= 0, hub_at, shifted)

    def build(block, carry):
        first = pl.multiple_of(block * BUILD, BUILD)
        ids = lax.broadcasted_iota(jnp.int32, (BUILD, rows), 0) + first
        total = jnp.zeros((BUILD, rows), F32)
        for k in range(K):
            total = total + jnp.where(place[k : k + 1] == ids, 1.0, 0.0)
        counts[pl.ds(first, BUILD)] = total.astype(BF16)
        return carry

    lax.fori_loop(0, counts.shape[0] // BUILD, build, 0)

    turned = jnp.transpose(perturb_f32)
    for g in range(feats):
        perturb_t[g] = turned[g * (width // feats) : (g + 1) * (width // feats)]
    perturbed_t = jnp.transpose(perturbed.astype(F32)).astype(BF16)
    summed_t = dot(perturbed_t, counts[0:rows], NN)
    preact_self = dot(perturbed, w_self[...], NN) + bias[...]

    for load in loads[7:9]:
        load.wait()
    for o in range(NOFF):
        halo_copy(o).wait_recv()
    each(doms - 1, lambda step: hub_recv(step).wait_recv())
    remote = jnp.concatenate(
        [halo_in[...].astype(F32).reshape(halo_rows, width), hub_in[...].reshape(-1, width)], 0
    )
    remote_t = jnp.transpose(remote).astype(BF16)
    summed_t = summed_t + dot(remote_t, counts[rows:], NN)
    mean_t = summed_t / K
    mean = jnp.transpose(mean_t).astype(BF16)
    preact = preact_self + dot(mean, w_neigh[...], NN)
    sigmoid_pre = jax.nn.sigmoid(preact)
    grad_pre = (
        upstream[...].astype(F32) * sigmoid_pre * (1.0 + preact * (1.0 - sigmoid_pre))
    ).astype(BF16)

    spread_t = halves(dot(w_neigh[...], grad_pre, NT) / K, 0)
    back = dot(counts[rows:], spread_t, NT)
    back = back[:, 0:width] + back[:, width:]
    for o in range(NOFF):
        back_out[o] = back[o * slot_pad : (o + 1) * slot_pad]
    hubg_out[...] = back[halo_rows:].reshape(hubg_out.shape)

    def back_copy(o):
        return copy_to(
            back_out.at[o], back_in.at[o], back_s.at[o], back_r.at[o], at_offset(-offset_of(o)), col
        )

    def hubg_send(step):
        peer = dom_peer(step)
        return copy_to(
            hubg_out.at[peer], hubg_in.at[me], hubg_s.at[peer], hubg_r.at[me], peer, col
        )

    def hubg_recv(step):
        peer = dom_peer(step)
        return copy_to(
            hubg_out.at[peer], hubg_in.at[peer], hubg_s.at[peer], hubg_r.at[peer], peer, col
        )

    for o in range(NOFF):
        back_copy(o).start()
    each(doms - 1, lambda step: hubg_send(step).start())

    both_t = jnp.concatenate([perturbed_t, mean_t.astype(BF16)], 0)
    weight_grads = dot(both_t, grad_pre, NN)
    for i in range(owners):
        part_out[i] = weight_grads[i * chunk : (i + 1) * chunk]

    def on_owner(dom, body):
        if owners == doms:
            body()
        else:
            pl.when(dom < owners)(body)

    def part_send(step):
        peer = dom_peer(step)
        return copy_to(part_out.at[peer], part_in.at[me], part_s.at[peer], part_r.at[me], peer, col)

    def part_recv(step):
        peer = dom_peer(step)
        return copy_to(part_out.at[0], part_in.at[peer], part_s.at[peer], part_r.at[peer], peer, col)

    def whole_send(step):
        peer = dom_peer(step)
        return copy_to(whole.at[me], whole.at[me], whole_s.at[peer], whole_r.at[me], peer, col)

    def whole_recv(step):
        peer = dom_peer(step)
        return copy_to(whole.at[peer], whole.at[peer], whole_s.at[peer], whole_r.at[peer], peer, col)

    each(doms - 1, lambda step: on_owner(dom_peer(step), lambda: part_send(step).start()))

    local = dot(spread_t, counts[0:rows], NT)
    grad_t = dot(w_self[...], grad_pre, NT) + local[0:width] + local[width:]

    for o in range(NOFF):
        back_copy(o).wait_recv()
    each(doms - 1, lambda step: hubg_recv(step).wait_recv())
    hubg_in[me] = hubg_out[me]
    hub_sum = jnp.sum(hubg_in[...], 0)
    hub_sum = jnp.concatenate([hub_sum, jnp.zeros((ROW_TILE - HUB_SLOT, width), F32)], 0)
    returned_t = halves(jnp.transpose(back_in[...].reshape(halo_rows, width)), 0)
    hub_sum_t = halves(jnp.transpose(hub_sum), 0)
    added = dot(returned_t, pick_halo, NN) + dot(hub_sum_t, pick_hub, NN)
    grad_t = grad_t + added[0:width] + added[width:]
    part_width = width // feats
    for g in range(feats):
        cols_out[g] = grad_t[g * part_width : (g + 1) * part_width]

    def cols_send(step):
        peer = feat_peer(step)
        return copy_to(cols_out.at[peer], cols_in.at[col], cols_s.at[peer], cols_r.at[col], me, peer)

    def cols_recv(step):
        peer = feat_peer(step)
        return copy_to(
            cols_out.at[peer], cols_in.at[peer], cols_s.at[peer], cols_r.at[peer], me, peer
        )

    each(feats - 1, lambda step: cols_send(step).start())

    def sum_parts():
        each(doms - 1, lambda step: part_recv(step).wait_recv())
        part_in[me] = part_out[me]
        whole[me] = jnp.sum(part_in[...], 0)
        each(doms - 1, lambda step: whole_send(step).start())

    on_owner(me, sum_parts)

    each(feats - 1, lambda step: cols_recv(step).wait_recv())
    cols_in[col] = cols_out[col]
    grad_cols = jnp.sum(cols_in[...], 0)
    square = jnp.sum(grad_cols * grad_cols, 0, keepdims=True)
    sq_out[...] = jnp.broadcast_to(square, sq_out.shape)

    def sq_send(step):
        peer = feat_peer(step)
        return copy_to(sq_out, sq_in.at[col], sq_s.at[peer], sq_r.at[col], me, peer)

    def sq_recv(step):
        peer = feat_peer(step)
        return copy_to(sq_out, sq_in.at[peer], sq_s.at[peer], sq_r.at[peer], me, peer)

    each(feats - 1, lambda step: sq_send(step).start())
    each(feats - 1, lambda step: sq_recv(step).wait_recv())
    sq_in[col] = sq_out[...]
    mean_square = jnp.sum(sq_in[...], 0)[0:1] / width
    stepped = perturb_t[col] + 0.5 * grad_cols / jnp.sqrt(mean_square + 1e-06)
    finish(new_perturb, stepped)

    def take_whole(step):
        on_owner(dom_peer(step), lambda: whole_recv(step).wait_recv())

    each(doms - 1, take_whole)
    half = owners // 2
    grad_self[...] = whole[0:half].reshape(grad_self.shape)
    grad_neigh[...] = whole[half:owners].reshape(grad_neigh.shape)

    for o in range(NOFF):
        halo_copy(o).wait_send()
        back_copy(o).wait_send()
    each(doms - 1, lambda step: hub_send(step).wait_send())
    each(doms - 1, lambda step: hubg_send(step).wait_send())
    each(doms - 1, lambda step: on_owner(dom_peer(step), lambda: part_send(step).wait_send()))
    on_owner(me, lambda: each(doms - 1, lambda step: whole_send(step).wait_send()))
    each(feats - 1, lambda step: cols_send(step).wait_send())
    each(feats - 1, lambda step: sq_send(step).wait_send())


def finish(new_perturb, stepped):
    new_perturb[...] = stepped.astype(BF16)


def per_device(
    doms, feats, features, perturb, w_self, w_neigh, bias, upstream, hub_rows, send_rows, neighbors
):
    rows, width = features.shape
    hidden = w_self.shape[1]
    slots = send_rows.shape[2]
    slot_pad = (slots + ROW_TILE - 1) // ROW_TILE * ROW_TILE
    chunk = max(8, 2 * width // doms)
    owners = 2 * width // chunk
    table = rows + NOFF * slot_pad + doms * HUB_SLOT
    part_width = width // feats
    hbm = pl.BlockSpec(memory_space=pltpu.HBM)
    vmem = pl.BlockSpec(memory_space=pltpu.VMEM)
    sems = pltpu.SemaphoreType.DMA
    scratch = [
        pltpu.VMEM((8, 128), jnp.int32),
        pltpu.VMEM((table, rows), BF16),
        pltpu.VMEM((feats, part_width, rows), F32),
        pltpu.VMEM((NOFF, slot_pad, width), BF16),
        pltpu.VMEM((NOFF, slot_pad, width), BF16),
        pltpu.VMEM((HUB_SLOT, width), F32),
        pltpu.VMEM((doms, HUB_SLOT, width), F32),
        pltpu.VMEM((NOFF, slot_pad, width), F32),
        pltpu.VMEM((NOFF, slot_pad, width), F32),
        pltpu.VMEM((doms, HUB_SLOT, width), F32),
        pltpu.VMEM((doms, HUB_SLOT, width), F32),
        pltpu.VMEM((owners, chunk, hidden), F32),
        pltpu.VMEM((doms, chunk, hidden), F32),
        pltpu.VMEM((owners, chunk, hidden), F32),
        pltpu.VMEM((feats, part_width, rows), F32),
        pltpu.VMEM((feats, part_width, rows), F32),
        pltpu.VMEM((8, rows), F32),
        pltpu.VMEM((feats, 8, rows), F32),
        sems((NOFF,)),
        sems((NOFF,)),
        sems((doms,)),
        sems((doms,)),
        sems((NOFF,)),
        sems((NOFF,)),
        sems((doms,)),
        sems((doms,)),
        sems((doms,)),
        sems((doms,)),
        sems((doms,)),
        sems((doms,)),
        sems((feats,)),
        sems((feats,)),
        sems((feats,)),
        sems((feats,)),
    ]
    args = (
        features,
        perturb,
        send_rows,
        hub_rows,
        neighbors.T,
        w_self,
        bias.reshape(1, hidden),
        w_neigh,
        upstream,
    )
    scratch += [pltpu.VMEM(x.shape, x.dtype) for x in args] + [sems((len(args),))]
    new_t, grad_self, grad_neigh = pl.pallas_call(
        functools.partial(kernel, doms, feats, owners, slots),
        out_shape=(
            jax.ShapeDtypeStruct((part_width, rows), BF16),
            jax.ShapeDtypeStruct((width, hidden), F32),
            jax.ShapeDtypeStruct((width, hidden), F32),
        ),
        in_specs=[hbm] * 9,
        out_specs=(vmem,) * 3,
        scratch_shapes=scratch,
        compiler_params=pltpu.CompilerParams(
            collective_id=0, has_side_effects=True, vmem_limit_bytes=60 * 2**20
        ),
    )(*args)
    return new_t.T, grad_self, grad_neigh


def solution(mesh):
    in_specs = (
        P("dom", None),
        P("dom", None),
        P(None, "feat"),
        P(None, "feat"),
        P("feat"),
        P("dom", "feat"),
        P("dom", None),
        P("dom", None, None),
        P("dom", None),
    )
    out_specs = (P("dom", "feat"), P(None, "feat"), P(None, "feat"))
    return jax.shard_map(
        functools.partial(per_device, mesh.shape["dom"], mesh.shape["feat"]),
        mesh=mesh,
        in_specs=in_specs,
        out_specs=out_specs,
        check_vma=False,
    )
```

```python
import functools

import jax
import jax.numpy as jnp
from jax import lax
from jax.experimental import pallas as pl
from jax.experimental.pallas import tpu as pltpu
from jax.sharding import PartitionSpec as P

K = 15
NOFF = 4
HUB_SLOT = 8
ROW_TILE = 16
BUILD = 32
MESH = pl.DeviceIdType.MESH
F32 = jnp.float32
BF16 = jnp.bfloat16


def offset_of(direction):
    return direction - 2 if direction < 2 else direction - 1


def dot(left, right, dims):
    return lax.dot_general(left, right, (dims, ((), ())), preferred_element_type=F32)


NN = ((1,), (0,))
NT = ((1,), (1,))


def halves(value, axis):
    high = value.astype(BF16)
    low = (value - high.astype(F32)).astype(BF16)
    return jnp.concatenate([high, low], axis)


def each(count, body):
    if count <= 8:
        for step in range(count):
            body(step)
    else:

        def run(step, carry):
            body(step)
            return carry

        lax.fori_loop(0, count, run, 0)


def kernel(
    doms,
    feats,
    owners,
    slots,
    features_far,
    perturb_far,
    send_rows_far,
    hub_rows_far,
    neighbors_far,
    w_self_far,
    bias_far,
    w_neigh_far,
    upstream_far,
    new_perturb,
    grad_self,
    grad_neigh,
    lists,
    counts,
    perturb_t,
    halo_out,
    halo_in,
    hub_out,
    hub_in,
    back_out,
    back_in,
    hubg_out,
    hubg_in,
    part_out,
    part_in,
    pair_in,
    pair_sum,
    whole,
    cols_out,
    cols_in,
    sq_out,
    sq_in,
    halo_s,
    halo_r,
    hub_s,
    hub_r,
    back_s,
    back_r,
    hubg_s,
    hubg_r,
    part_s,
    part_r,
    pair_r,
    whole_s,
    whole_r,
    cols_s,
    cols_r,
    sq_s,
    sq_r,
    features,
    perturb,
    send_rows,
    hub_rows,
    neighbors,
    w_self,
    bias,
    w_neigh,
    upstream,
    load_s,
):
    far = (
        features_far,
        perturb_far,
        send_rows_far,
        hub_rows_far,
        neighbors_far,
        w_self_far,
        bias_far,
        w_neigh_far,
        upstream_far,
    )
    near = (features, perturb, send_rows, hub_rows, neighbors, w_self, bias, w_neigh, upstream)
    loads = [
        pltpu.make_async_copy(there, here, load_s.at[i])
        for i, (there, here) in enumerate(zip(far, near))
    ]
    for load in loads:
        load.start()
    me = lax.axis_index("dom")
    col = lax.axis_index("feat")
    rows, width = features.shape
    slot_pad = halo_out.shape[1]
    halo_rows = NOFF * slot_pad
    chunk = part_out.shape[1]

    def dom_peer(step):
        return lax.rem(me + step + 1, doms)

    def feat_peer(step):
        return lax.rem(col + step + 1, feats)

    def at_offset(by):
        return lax.rem(me + by + doms, doms)

    barrier = pltpu.get_barrier_semaphore()

    def greet_dom(step):
        pl.semaphore_signal(
            barrier, inc=1, device_id=(dom_peer(step), col), device_id_type=MESH
        )

    def greet_feat(step):
        pl.semaphore_signal(
            barrier, inc=1, device_id=(me, feat_peer(step)), device_id_type=MESH
        )

    each(doms - 1, greet_dom)
    each(feats - 1, greet_feat)

    def copy_to(src, dst, send, recv, dom, feat):
        return pltpu.make_async_remote_copy(
            src_ref=src,
            dst_ref=dst,
            send_sem=send,
            recv_sem=recv,
            device_id=(dom, feat),
            device_id_type=MESH,
        )

    for load in loads[0:4]:
        load.wait()
    perturb_f32 = perturb[...].astype(F32)
    perturbed = (features[...].astype(F32) + perturb_f32).astype(BF16)
    lists[...] = jnp.full(lists.shape, -1, jnp.int32)
    lists[0:NOFF, 0:slots] = send_rows[0]
    lists[NOFF : NOFF + 1, 0 : hub_rows.shape[1]] = hub_rows[...]
    by_slot = jnp.transpose(lists[...].astype(F32))
    row_ids = lax.broadcasted_iota(jnp.int32, (slot_pad, rows), 1).astype(F32)
    picks = [
        jnp.where(by_slot[0:slot_pad, o : o + 1] == row_ids, 1.0, 0.0).astype(BF16)
        for o in range(NOFF)
    ]
    pick_halo = jnp.concatenate(picks, 0)
    pick_hub = jnp.where(
        by_slot[0:ROW_TILE, NOFF : NOFF + 1] == row_ids[0:ROW_TILE], 1.0, 0.0
    ).astype(BF16)
    picked = dot(pick_halo, perturbed, NN).astype(BF16)
    for o in range(NOFF):
        halo_out[o] = picked[o * slot_pad : (o + 1) * slot_pad]
    own_hubs = dot(pick_hub, perturbed, NN)[0:HUB_SLOT]
    hub_out[...] = own_hubs
    hub_in[me] = own_hubs

    pl.semaphore_wait(barrier, doms - 1 + feats - 1)

    def halo_copy(o):
        return copy_to(
            halo_out.at[o], halo_in.at[o], halo_s.at[o], halo_r.at[o], at_offset(offset_of(o)), col
        )

    def hub_send(step):
        peer = dom_peer(step)
        return copy_to(hub_out, hub_in.at[me], hub_s.at[peer], hub_r.at[me], peer, col)

    def hub_recv(step):
        peer = dom_peer(step)
        return copy_to(hub_out, hub_in.at[peer], hub_s.at[peer], hub_r.at[peer], peer, col)

    for o in range(NOFF):
        halo_copy(o).start()
    each(doms - 1, lambda step: hub_send(step).start())

    for load in loads[4:7]:
        load.wait()
    nodes = neighbors[...]
    beyond = nodes - rows
    shifted = nodes
    for o in range(1, NOFF):
        shifted = shifted + jnp.where(beyond >= o * slots, slot_pad - slots, 0)
    hub_id = beyond - NOFF * slots
    hub_at = rows + halo_rows + (hub_id >> 1) * HUB_SLOT + (hub_id & 1)
    place = jnp.where(hub_id >= 0, hub_at, shifted)

    def build(block, carry):
        first = pl.multiple_of(block * BUILD, BUILD)
        ids = lax.broadcasted_iota(jnp.int32, (BUILD, rows), 0) + first
        total = jnp.zeros((BUILD, rows), F32)
        for k in range(K):
            total = total + jnp.where(place[k : k + 1] == ids, 1.0, 0.0)
        counts[pl.ds(first, BUILD)] = total.astype(BF16)
        return carry

    lax.fori_loop(0, counts.shape[0] // BUILD, build, 0)

    turned = jnp.transpose(perturb_f32)
    for g in range(feats):
        perturb_t[g] = turned[g * (width // feats) : (g + 1) * (width // feats)]
    perturbed_t = jnp.transpose(perturbed.astype(F32)).astype(BF16)
    summed_t = dot(perturbed_t, counts[0:rows], NN)
    preact_self = dot(perturbed, w_self[...], NN) + bias[...]

    for load in loads[7:9]:
        load.wait()
    for o in range(NOFF):
        halo_copy(o).wait_recv()
    each(doms - 1, lambda step: hub_recv(step).wait_recv())
    remote = jnp.concatenate(
        [halo_in[...].astype(F32).reshape(halo_rows, width), hub_in[...].reshape(-1, width)], 0
    )
    remote_t = jnp.transpose(remote).astype(BF16)
    summed_t = summed_t + dot(remote_t, counts[rows:], NN)
    mean_t = summed_t / K
    mean = jnp.transpose(mean_t).astype(BF16)
    preact = preact_self + dot(mean, w_neigh[...], NN)
    sigmoid_pre = jax.nn.sigmoid(preact)
    grad_pre = (
        upstream[...].astype(F32) * sigmoid_pre * (1.0 + preact * (1.0 - sigmoid_pre))
    ).astype(BF16)

    spread_t = halves(dot(w_neigh[...], grad_pre, NT) / K, 0)
    back = dot(counts[rows:], spread_t, NT)
    back = back[:, 0:width] + back[:, width:]
    for o in range(NOFF):
        back_out[o] = back[o * slot_pad : (o + 1) * slot_pad]
    hubg_out[...] = back[halo_rows:].reshape(hubg_out.shape)

    def back_copy(o):
        return copy_to(
            back_out.at[o], back_in.at[o], back_s.at[o], back_r.at[o], at_offset(-offset_of(o)), col
        )

    def hubg_send(step):
        peer = dom_peer(step)
        return copy_to(
            hubg_out.at[peer], hubg_in.at[me], hubg_s.at[peer], hubg_r.at[me], peer, col
        )

    def hubg_recv(step):
        peer = dom_peer(step)
        return copy_to(
            hubg_out.at[peer], hubg_in.at[peer], hubg_s.at[peer], hubg_r.at[peer], peer, col
        )

    for o in range(NOFF):
        back_copy(o).start()
    each(doms - 1, lambda step: hubg_send(step).start())

    both_t = jnp.concatenate([perturbed_t, mean_t.astype(BF16)], 0)
    weight_grads = dot(both_t, grad_pre, NN)
    for i in range(owners):
        part_out[i] = weight_grads[i * chunk : (i + 1) * chunk]

    def on_owner(dom, body):
        if owners == doms:
            body()
        else:
            pl.when(dom < owners)(body)

    flip = 1 - 2 * lax.rem(me, 2)
    partner = me + flip

    def same(step):
        return lax.rem(me + 2 * step, doms)

    def pair_send(step):
        peer = same(step) + flip
        return copy_to(part_out.at[peer], pair_in.at[peer], part_s.at[peer], pair_r.at[peer], partner, col)

    def pair_recv(step):
        peer = same(step)
        return copy_to(part_out.at[peer], pair_in.at[peer], part_s.at[peer], pair_r.at[peer], partner, col)

    def part_send(step):
        peer = same(step)
        return copy_to(pair_sum.at[peer], part_in.at[me], part_s.at[peer], part_r.at[me], peer, col)

    def part_recv(step):
        peer = same(step)
        return copy_to(pair_sum.at[0], part_in.at[peer], part_s.at[peer], part_r.at[peer], peer, col)

    def whole_send(step):
        peer = same(step)
        return copy_to(whole.at[me], whole.at[me], whole_s.at[peer], whole_r.at[me], peer, col)

    def whole_recv(peer):
        return copy_to(whole.at[peer], whole.at[peer], whole_s.at[peer], whole_r.at[peer], peer, col)

    def pass_on(step):
        peer = same(step)
        return copy_to(
            whole.at[peer], whole.at[peer], whole_s.at[peer + flip], whole_r.at[peer], partner, col
        )

    pairs = doms // 2
    each(pairs, lambda step: on_owner(same(step), lambda: pair_send(step).start()))

    local = dot(spread_t, counts[0:rows], NT)
    grad_t = dot(w_self[...], grad_pre, NT) + local[0:width] + local[width:]

    for o in range(NOFF):
        back_copy(o).wait_recv()
    each(doms - 1, lambda step: hubg_recv(step).wait_recv())

    def add_pair(step):
        peer = same(step)

        def run():
            pair_recv(step).wait_recv()
            pair_sum[peer] = part_out[peer] + pair_in[peer]

        on_owner(peer, run)

    each(pairs, add_pair)
    each(pairs - 1, lambda step: on_owner(same(step + 1), lambda: part_send(step + 1).start()))
    hubg_in[me] = hubg_out[me]
    hub_sum = jnp.sum(hubg_in[...], 0)
    hub_sum = jnp.concatenate([hub_sum, jnp.zeros((ROW_TILE - HUB_SLOT, width), F32)], 0)
    returned_t = halves(jnp.transpose(back_in[...].reshape(halo_rows, width)), 0)
    hub_sum_t = halves(jnp.transpose(hub_sum), 0)
    added = dot(returned_t, pick_halo, NN) + dot(hub_sum_t, pick_hub, NN)
    grad_t = grad_t + added[0:width] + added[width:]
    part_width = width // feats
    for g in range(feats):
        cols_out[g] = grad_t[g * part_width : (g + 1) * part_width]

    def cols_send(step):
        peer = feat_peer(step)
        return copy_to(cols_out.at[peer], cols_in.at[col], cols_s.at[peer], cols_r.at[col], me, peer)

    def cols_recv(step):
        peer = feat_peer(step)
        return copy_to(
            cols_out.at[peer], cols_in.at[peer], cols_s.at[peer], cols_r.at[peer], me, peer
        )

    each(feats - 1, lambda step: cols_send(step).start())

    def sum_parts():
        each(pairs - 1, lambda step: part_recv(step + 1).wait_recv())
        total = pair_sum[me]
        for step in range(pairs - 1):
            total = total + part_in[same(step + 1)]
        whole[me] = total
        each(pairs - 1, lambda step: whole_send(step + 1).start())
        pass_on(0).start()

    on_owner(me, sum_parts)

    each(feats - 1, lambda step: cols_recv(step).wait_recv())
    cols_in[col] = cols_out[col]
    grad_cols = jnp.sum(cols_in[...], 0)
    square = jnp.sum(grad_cols * grad_cols, 0, keepdims=True)
    sq_out[...] = jnp.broadcast_to(square, sq_out.shape)

    def sq_send(step):
        peer = feat_peer(step)
        return copy_to(sq_out, sq_in.at[col], sq_s.at[peer], sq_r.at[col], me, peer)

    def sq_recv(step):
        peer = feat_peer(step)
        return copy_to(sq_out, sq_in.at[peer], sq_s.at[peer], sq_r.at[peer], me, peer)

    each(feats - 1, lambda step: sq_send(step).start())

    def forward(step):
        def run():
            whole_recv(same(step + 1)).wait_recv()
            pass_on(step + 1).start()

        on_owner(same(step + 1), run)

    each(pairs - 1, forward)
    each(feats - 1, lambda step: sq_recv(step).wait_recv())
    sq_in[col] = sq_out[...]
    mean_square = jnp.sum(sq_in[...], 0)[0:1] / width
    stepped = perturb_t[col] + 0.5 * grad_cols / jnp.sqrt(mean_square + 1e-06)
    finish(new_perturb, stepped)

    def take_whole(step):
        peer = same(step) + flip
        on_owner(peer, lambda: whole_recv(peer).wait_recv())

    each(pairs, take_whole)
    half = owners // 2
    grad_self[...] = whole[0:half].reshape(grad_self.shape)
    grad_neigh[...] = whole[half:owners].reshape(grad_neigh.shape)

    for o in range(NOFF):
        halo_copy(o).wait_send()
        back_copy(o).wait_send()
    each(doms - 1, lambda step: hub_send(step).wait_send())
    each(doms - 1, lambda step: hubg_send(step).wait_send())
    each(pairs, lambda step: on_owner(same(step), lambda: pair_send(step).wait_send()))
    each(pairs - 1, lambda step: on_owner(same(step + 1), lambda: part_send(step + 1).wait_send()))
    on_owner(me, lambda: each(pairs - 1, lambda step: whole_send(step + 1).wait_send()))
    each(pairs, lambda step: on_owner(same(step), lambda: pass_on(step).wait_send()))
    each(feats - 1, lambda step: cols_send(step).wait_send())
    each(feats - 1, lambda step: sq_send(step).wait_send())


def finish(new_perturb, stepped):
    new_perturb[...] = stepped.astype(BF16)


def per_device(
    doms, feats, features, perturb, w_self, w_neigh, bias, upstream, hub_rows, send_rows, neighbors
):
    rows, width = features.shape
    hidden = w_self.shape[1]
    slots = send_rows.shape[2]
    slot_pad = (slots + ROW_TILE - 1) // ROW_TILE * ROW_TILE
    chunk = max(8, 2 * width // doms)
    owners = 2 * width // chunk
    table = rows + NOFF * slot_pad + doms * HUB_SLOT
    part_width = width // feats
    hbm = pl.BlockSpec(memory_space=pltpu.HBM)
    vmem = pl.BlockSpec(memory_space=pltpu.VMEM)
    sems = pltpu.SemaphoreType.DMA
    scratch = [
        pltpu.VMEM((8, 128), jnp.int32),
        pltpu.VMEM((table, rows), BF16),
        pltpu.VMEM((feats, part_width, rows), F32),
        pltpu.VMEM((NOFF, slot_pad, width), BF16),
        pltpu.VMEM((NOFF, slot_pad, width), BF16),
        pltpu.VMEM((HUB_SLOT, width), F32),
        pltpu.VMEM((doms, HUB_SLOT, width), F32),
        pltpu.VMEM((NOFF, slot_pad, width), F32),
        pltpu.VMEM((NOFF, slot_pad, width), F32),
        pltpu.VMEM((doms, HUB_SLOT, width), F32),
        pltpu.VMEM((doms, HUB_SLOT, width), F32),
        pltpu.VMEM((owners, chunk, hidden), F32),
        pltpu.VMEM((doms, chunk, hidden), F32),
        pltpu.VMEM((owners, chunk, hidden), F32),
        pltpu.VMEM((owners, chunk, hidden), F32),
        pltpu.VMEM((owners, chunk, hidden), F32),
        pltpu.VMEM((feats, part_width, rows), F32),
        pltpu.VMEM((feats, part_width, rows), F32),
        pltpu.VMEM((8, rows), F32),
        pltpu.VMEM((feats, 8, rows), F32),
        sems((NOFF,)),
        sems((NOFF,)),
        sems((doms,)),
        sems((doms,)),
        sems((NOFF,)),
        sems((NOFF,)),
        sems((doms,)),
        sems((doms,)),
        sems((doms,)),
        sems((doms,)),
        sems((doms,)),
        sems((doms,)),
        sems((doms,)),
        sems((feats,)),
        sems((feats,)),
        sems((feats,)),
        sems((feats,)),
    ]
    args = (
        features,
        perturb,
        send_rows,
        hub_rows,
        neighbors.T,
        w_self,
        bias.reshape(1, hidden),
        w_neigh,
        upstream,
    )
    scratch += [pltpu.VMEM(x.shape, x.dtype) for x in args] + [sems((len(args),))]
    new_t, grad_self, grad_neigh = pl.pallas_call(
        functools.partial(kernel, doms, feats, owners, slots),
        out_shape=(
            jax.ShapeDtypeStruct((part_width, rows), BF16),
            jax.ShapeDtypeStruct((width, hidden), F32),
            jax.ShapeDtypeStruct((width, hidden), F32),
        ),
        in_specs=[hbm] * 9,
        out_specs=(vmem,) * 3,
        scratch_shapes=scratch,
        compiler_params=pltpu.CompilerParams(
            collective_id=0, has_side_effects=True, vmem_limit_bytes=60 * 2**20
        ),
    )(*args)
    return new_t.T, grad_self, grad_neigh


def solution(mesh):
    in_specs = (
        P("dom", None),
        P("dom", None),
        P(None, "feat"),
        P(None, "feat"),
        P("feat"),
        P("dom", "feat"),
        P("dom", None),
        P("dom", None, None),
        P("dom", None),
    )
    out_specs = (P("dom", "feat"), P(None, "feat"), P(None, "feat"))
    return jax.shard_map(
        functools.partial(per_device, mesh.shape["dom"], mesh.shape["feat"]),
        mesh=mesh,
        in_specs=in_specs,
        out_specs=out_specs,
        check_vma=False,
    )
```

```python
import functools

import jax
import jax.numpy as jnp
from jax import lax
from jax.experimental import pallas as pl
from jax.experimental.pallas import tpu as pltpu
from jax.sharding import PartitionSpec as P

K = 15
NOFF = 4
HUB_SLOT = 8
ROW_TILE = 16
BUILD = 32
MESH = pl.DeviceIdType.MESH
F32 = jnp.float32
BF16 = jnp.bfloat16


def offset_of(direction):
    return direction - 2 if direction < 2 else direction - 1


def dot(left, right, dims):
    return lax.dot_general(left, right, (dims, ((), ())), preferred_element_type=F32)


NN = ((1,), (0,))
NT = ((1,), (1,))


def halves(value, axis):
    high = value.astype(BF16)
    low = (value - high.astype(F32)).astype(BF16)
    return jnp.concatenate([high, low], axis)


def each(count, body):
    if count <= 8:
        for step in range(count):
            body(step)
    else:

        def run(step, carry):
            body(step)
            return carry

        lax.fori_loop(0, count, run, 0)


def kernel(
    doms,
    feats,
    owners,
    slots,
    features_far,
    perturb_far,
    send_rows_far,
    hub_rows_far,
    neighbors_far,
    w_self_far,
    bias_far,
    w_neigh_far,
    upstream_far,
    new_perturb,
    grad_self,
    grad_neigh,
    lists,
    counts,
    perturb_t,
    halo_out,
    halo_in,
    hub_out,
    hub_in,
    back_out,
    back_in,
    hubg_out,
    hubg_in,
    part_out,
    part_in,
    whole,
    cols_out,
    cols_in,
    sq_out,
    sq_in,
    halo_s,
    halo_r,
    hub_s,
    hub_r,
    back_s,
    back_r,
    hubg_s,
    hubg_r,
    part_s,
    part_r,
    whole_s,
    whole_r,
    cols_s,
    cols_r,
    sq_s,
    sq_r,
    features,
    perturb,
    send_rows,
    hub_rows,
    neighbors,
    w_self,
    bias,
    w_neigh,
    upstream,
    load_s,
    new_near,
    store_s,
):
    far = (
        features_far,
        perturb_far,
        send_rows_far,
        hub_rows_far,
        neighbors_far,
        w_self_far,
        bias_far,
        w_neigh_far,
        upstream_far,
    )
    near = (features, perturb, send_rows, hub_rows, neighbors, w_self, bias, w_neigh, upstream)
    loads = [
        pltpu.make_async_copy(there, here, load_s.at[i])
        for i, (there, here) in enumerate(zip(far, near))
    ]
    for load in loads:
        load.start()
    me = lax.axis_index("dom")
    col = lax.axis_index("feat")
    rows, width = features.shape
    slot_pad = halo_out.shape[1]
    halo_rows = NOFF * slot_pad
    chunk = part_out.shape[1]

    def dom_peer(step):
        return lax.rem(me + step + 1, doms)

    def feat_peer(step):
        return lax.rem(col + step + 1, feats)

    def at_offset(by):
        return lax.rem(me + by + doms, doms)

    barrier = pltpu.get_barrier_semaphore()

    def greet_dom(step):
        pl.semaphore_signal(
            barrier, inc=1, device_id=(dom_peer(step), col), device_id_type=MESH
        )

    def greet_feat(step):
        pl.semaphore_signal(
            barrier, inc=1, device_id=(me, feat_peer(step)), device_id_type=MESH
        )

    each(doms - 1, greet_dom)
    each(feats - 1, greet_feat)

    def copy_to(src, dst, send, recv, dom, feat):
        return pltpu.make_async_remote_copy(
            src_ref=src,
            dst_ref=dst,
            send_sem=send,
            recv_sem=recv,
            device_id=(dom, feat),
            device_id_type=MESH,
        )

    for load in loads[0:4]:
        load.wait()
    perturb_f32 = perturb[...].astype(F32)
    perturbed = (features[...].astype(F32) + perturb_f32).astype(BF16)
    lists[...] = jnp.full(lists.shape, -1, jnp.int32)
    lists[0:NOFF, 0:slots] = send_rows[0]
    lists[NOFF : NOFF + 1, 0 : hub_rows.shape[1]] = hub_rows[...]
    by_slot = jnp.transpose(lists[...].astype(F32))
    row_ids = lax.broadcasted_iota(jnp.int32, (slot_pad, rows), 1).astype(F32)
    picks = [
        jnp.where(by_slot[0:slot_pad, o : o + 1] == row_ids, 1.0, 0.0).astype(BF16)
        for o in range(NOFF)
    ]
    pick_halo = jnp.concatenate(picks, 0)
    pick_hub = jnp.where(
        by_slot[0:ROW_TILE, NOFF : NOFF + 1] == row_ids[0:ROW_TILE], 1.0, 0.0
    ).astype(BF16)
    picked = dot(pick_halo, perturbed, NN).astype(BF16)
    for o in range(NOFF):
        halo_out[o] = picked[o * slot_pad : (o + 1) * slot_pad]
    own_hubs = dot(pick_hub, perturbed, NN)[0:HUB_SLOT]
    hub_out[...] = own_hubs
    hub_in[me] = own_hubs

    pl.semaphore_wait(barrier, doms - 1 + feats - 1)

    def halo_copy(o):
        return copy_to(
            halo_out.at[o], halo_in.at[o], halo_s.at[o], halo_r.at[o], at_offset(offset_of(o)), col
        )

    def hub_send(step):
        peer = dom_peer(step)
        return copy_to(hub_out, hub_in.at[me], hub_s.at[peer], hub_r.at[me], peer, col)

    def hub_recv(step):
        peer = dom_peer(step)
        return copy_to(hub_out, hub_in.at[peer], hub_s.at[peer], hub_r.at[peer], peer, col)

    for o in range(NOFF):
        halo_copy(o).start()
    each(doms - 1, lambda step: hub_send(step).start())

    for load in loads[4:7]:
        load.wait()
    nodes = neighbors[...]
    beyond = nodes - rows
    shifted = nodes
    for o in range(1, NOFF):
        shifted = shifted + jnp.where(beyond >= o * slots, slot_pad - slots, 0)
    hub_id = beyond - NOFF * slots
    hub_at = rows + halo_rows + (hub_id >> 1) * HUB_SLOT + (hub_id & 1)
    place = jnp.where(hub_id >= 0, hub_at, shifted)

    def build(block, carry):
        first = pl.multiple_of(block * BUILD, BUILD)
        ids = lax.broadcasted_iota(jnp.int32, (BUILD, rows), 0) + first
        total = jnp.zeros((BUILD, rows), F32)
        for k in range(K):
            total = total + jnp.where(place[k : k + 1] == ids, 1.0, 0.0)
        counts[pl.ds(first, BUILD)] = total.astype(BF16)
        return carry

    lax.fori_loop(0, counts.shape[0] // BUILD, build, 0)

    turned = jnp.transpose(perturb_f32)
    for g in range(feats):
        perturb_t[g] = turned[g * (width // feats) : (g + 1) * (width // feats)]
    perturbed_t = jnp.transpose(perturbed.astype(F32)).astype(BF16)
    summed_t = dot(perturbed_t, counts[0:rows], NN)
    preact_self = dot(perturbed, w_self[...], NN) + bias[...]

    for load in loads[7:9]:
        load.wait()
    for o in range(NOFF):
        halo_copy(o).wait_recv()
    each(doms - 1, lambda step: hub_recv(step).wait_recv())
    remote = jnp.concatenate(
        [halo_in[...].astype(F32).reshape(halo_rows, width), hub_in[...].reshape(-1, width)], 0
    )
    remote_t = jnp.transpose(remote).astype(BF16)
    summed_t = summed_t + dot(remote_t, counts[rows:], NN)
    mean_t = summed_t / K
    mean = jnp.transpose(mean_t).astype(BF16)
    preact = preact_self + dot(mean, w_neigh[...], NN)
    sigmoid_pre = jax.nn.sigmoid(preact)
    grad_pre = (
        upstream[...].astype(F32) * sigmoid_pre * (1.0 + preact * (1.0 - sigmoid_pre))
    ).astype(BF16)

    spread_t = halves(dot(w_neigh[...], grad_pre, NT) / K, 0)
    back = dot(counts[rows:], spread_t, NT)
    back = back[:, 0:width] + back[:, width:]
    for o in range(NOFF):
        back_out[o] = back[o * slot_pad : (o + 1) * slot_pad]
    hubg_out[...] = back[halo_rows:].reshape(hubg_out.shape)

    def back_copy(o):
        return copy_to(
            back_out.at[o], back_in.at[o], back_s.at[o], back_r.at[o], at_offset(-offset_of(o)), col
        )

    def hubg_send(step):
        peer = dom_peer(step)
        return copy_to(
            hubg_out.at[peer], hubg_in.at[me], hubg_s.at[peer], hubg_r.at[me], peer, col
        )

    def hubg_recv(step):
        peer = dom_peer(step)
        return copy_to(
            hubg_out.at[peer], hubg_in.at[peer], hubg_s.at[peer], hubg_r.at[peer], peer, col
        )

    for o in range(NOFF):
        back_copy(o).start()
    each(doms - 1, lambda step: hubg_send(step).start())

    both_t = jnp.concatenate([perturbed_t, mean_t.astype(BF16)], 0)
    weight_grads = dot(both_t, grad_pre, NN)
    for i in range(owners):
        part_out[i] = weight_grads[i * chunk : (i + 1) * chunk]

    def on_owner(dom, body):
        if owners == doms:
            body()
        else:
            pl.when(dom < owners)(body)

    def part_send(step):
        peer = dom_peer(step)
        return copy_to(part_out.at[peer], part_in.at[me], part_s.at[peer], part_r.at[me], peer, col)

    def part_recv(step):
        peer = dom_peer(step)
        return copy_to(part_out.at[0], part_in.at[peer], part_s.at[peer], part_r.at[peer], peer, col)

    def whole_send(step):
        peer = dom_peer(step)
        return copy_to(whole.at[me], whole.at[me], whole_s.at[peer], whole_r.at[me], peer, col)

    each(doms - 1, lambda step: on_owner(dom_peer(step), lambda: part_send(step).start()))

    local = dot(spread_t, counts[0:rows], NT)
    grad_t = dot(w_self[...], grad_pre, NT) + local[0:width] + local[width:]

    for o in range(NOFF):
        back_copy(o).wait_recv()
    each(doms - 1, lambda step: hubg_recv(step).wait_recv())
    hubg_in[me] = hubg_out[me]
    hub_sum = jnp.sum(hubg_in[...], 0)
    hub_sum = jnp.concatenate([hub_sum, jnp.zeros((ROW_TILE - HUB_SLOT, width), F32)], 0)
    returned_t = halves(jnp.transpose(back_in[...].reshape(halo_rows, width)), 0)
    hub_sum_t = halves(jnp.transpose(hub_sum), 0)
    added = dot(returned_t, pick_halo, NN) + dot(hub_sum_t, pick_hub, NN)
    grad_t = grad_t + added[0:width] + added[width:]
    part_width = width // feats
    for g in range(feats):
        cols_out[g] = grad_t[g * part_width : (g + 1) * part_width]

    def cols_send(step):
        peer = feat_peer(step)
        return copy_to(cols_out.at[peer], cols_in.at[col], cols_s.at[peer], cols_r.at[col], me, peer)

    def cols_recv(step):
        peer = feat_peer(step)
        return copy_to(
            cols_out.at[peer], cols_in.at[peer], cols_s.at[peer], cols_r.at[peer], me, peer
        )

    each(feats - 1, lambda step: cols_send(step).start())

    def sum_parts():
        each(doms - 1, lambda step: part_recv(step).wait_recv())
        part_in[me] = part_out[me]
        whole[me] = jnp.sum(part_in[...], 0)
        each(doms - 1, lambda step: whole_send(step).start())

    on_owner(me, sum_parts)

    each(feats - 1, lambda step: cols_recv(step).wait_recv())
    cols_in[col] = cols_out[col]
    grad_cols = jnp.sum(cols_in[...], 0)
    square = jnp.sum(grad_cols * grad_cols, 0, keepdims=True)
    sq_out[...] = jnp.broadcast_to(square, sq_out.shape)

    def sq_send(step):
        peer = feat_peer(step)
        return copy_to(sq_out, sq_in.at[col], sq_s.at[peer], sq_r.at[col], me, peer)

    def sq_recv(step):
        peer = feat_peer(step)
        return copy_to(sq_out, sq_in.at[peer], sq_s.at[peer], sq_r.at[peer], me, peer)

    each(feats - 1, lambda step: sq_send(step).start())
    each(feats - 1, lambda step: sq_recv(step).wait_recv())
    sq_in[col] = sq_out[...]
    mean_square = jnp.sum(sq_in[...], 0)[0:1] / width
    stepped = perturb_t[col] + 0.5 * grad_cols / jnp.sqrt(mean_square + 1e-06)
    new_near[...] = stepped.astype(BF16)
    stores = [pltpu.make_async_copy(new_near, new_perturb, store_s.at[owners])]
    stores[0].start()

    half = owners // 2
    for i in range(owners):

        def arrive(i=i):
            copy_to(
                whole.at[i], whole.at[i], whole_s.at[i], whole_r.at[i], i, col
            ).wait_recv()

        pl.when(me != i)(arrive)
        target = grad_self if i < half else grad_neigh
        first = i % half * chunk
        stores.append(
            pltpu.make_async_copy(
                whole.at[i], target.at[first : first + chunk], store_s.at[i]
            )
        )
        stores[-1].start()
    for copy in stores:
        copy.wait()

    for o in range(NOFF):
        halo_copy(o).wait_send()
        back_copy(o).wait_send()
    each(doms - 1, lambda step: hub_send(step).wait_send())
    each(doms - 1, lambda step: hubg_send(step).wait_send())
    each(doms - 1, lambda step: on_owner(dom_peer(step), lambda: part_send(step).wait_send()))
    on_owner(me, lambda: each(doms - 1, lambda step: whole_send(step).wait_send()))
    each(feats - 1, lambda step: cols_send(step).wait_send())
    each(feats - 1, lambda step: sq_send(step).wait_send())


def per_device(
    doms, feats, features, perturb, w_self, w_neigh, bias, upstream, hub_rows, send_rows, neighbors
):
    rows, width = features.shape
    hidden = w_self.shape[1]
    slots = send_rows.shape[2]
    slot_pad = (slots + ROW_TILE - 1) // ROW_TILE * ROW_TILE
    chunk = max(8, 2 * width // doms)
    owners = 2 * width // chunk
    table = rows + NOFF * slot_pad + doms * HUB_SLOT
    part_width = width // feats
    hbm = pl.BlockSpec(memory_space=pltpu.HBM)
    sems = pltpu.SemaphoreType.DMA
    scratch = [
        pltpu.VMEM((8, 128), jnp.int32),
        pltpu.VMEM((table, rows), BF16),
        pltpu.VMEM((feats, part_width, rows), F32),
        pltpu.VMEM((NOFF, slot_pad, width), BF16),
        pltpu.VMEM((NOFF, slot_pad, width), BF16),
        pltpu.VMEM((HUB_SLOT, width), F32),
        pltpu.VMEM((doms, HUB_SLOT, width), F32),
        pltpu.VMEM((NOFF, slot_pad, width), F32),
        pltpu.VMEM((NOFF, slot_pad, width), F32),
        pltpu.VMEM((doms, HUB_SLOT, width), F32),
        pltpu.VMEM((doms, HUB_SLOT, width), F32),
        pltpu.VMEM((owners, chunk, hidden), F32),
        pltpu.VMEM((doms, chunk, hidden), F32),
        pltpu.VMEM((owners, chunk, hidden), F32),
        pltpu.VMEM((feats, part_width, rows), F32),
        pltpu.VMEM((feats, part_width, rows), F32),
        pltpu.VMEM((8, rows), F32),
        pltpu.VMEM((feats, 8, rows), F32),
        sems((NOFF,)),
        sems((NOFF,)),
        sems((doms,)),
        sems((doms,)),
        sems((NOFF,)),
        sems((NOFF,)),
        sems((doms,)),
        sems((doms,)),
        sems((doms,)),
        sems((doms,)),
        sems((doms,)),
        sems((doms,)),
        sems((feats,)),
        sems((feats,)),
        sems((feats,)),
        sems((feats,)),
    ]
    args = (
        features,
        perturb,
        send_rows,
        hub_rows,
        neighbors.T,
        w_self,
        bias.reshape(1, hidden),
        w_neigh,
        upstream,
    )
    scratch += [pltpu.VMEM(x.shape, x.dtype) for x in args] + [sems((len(args),))]
    scratch += [pltpu.VMEM((part_width, rows), BF16), sems((owners + 1,))]
    new_t, grad_self, grad_neigh = pl.pallas_call(
        functools.partial(kernel, doms, feats, owners, slots),
        out_shape=(
            jax.ShapeDtypeStruct((part_width, rows), BF16),
            jax.ShapeDtypeStruct((width, hidden), F32),
            jax.ShapeDtypeStruct((width, hidden), F32),
        ),
        in_specs=[hbm] * 9,
        out_specs=(hbm,) * 3,
        scratch_shapes=scratch,
        compiler_params=pltpu.CompilerParams(
            collective_id=0, has_side_effects=True, vmem_limit_bytes=60 * 2**20
        ),
    )(*args)
    return new_t.T, grad_self, grad_neigh


def solution(mesh):
    in_specs = (
        P("dom", None),
        P("dom", None),
        P(None, "feat"),
        P(None, "feat"),
        P("feat"),
        P("dom", "feat"),
        P("dom", None),
        P("dom", None, None),
        P("dom", None),
    )
    out_specs = (P("dom", "feat"), P(None, "feat"), P(None, "feat"))
    return jax.shard_map(
        functools.partial(per_device, mesh.shape["dom"], mesh.shape["feat"]),
        mesh=mesh,
        in_specs=in_specs,
        out_specs=out_specs,
        check_vma=False,
    )
```
